128 devices in a mesh: deg: 16 (over y, x), ord: 8 (over z, core).
Axes of the slice: x: 4, y: 4, z: 4, core: 2. Of those that a mesh axis runs over, the one named last changes fastest.
Arguments:
- coefficients: bfloat16 [2048, 2048, 128], P('ord', 'deg'), as said below
- legendre: bfloat16 [2048, 2048, 256], P('ord', 'deg'), as said below
- order_table: int32 [2048], replicated, may hold values from 0 to 2047, as said below
Outputs:
- products: bfloat16 [256, 32, 4096], P(('deg', 'ord'))
The draws below stay inside these ranges and needn't reach their ends.
Inputs may be any that keep to these rules, and one draw needn't show every extreme that they name: `order_table`: every order from 0 to 2047 appears once. For each index j of ord, with H = 128, the slots j * 256 to j * 256 + H - 1 hold orders below 1024, and slot j * 256 + H + s holds 2047 minus the order of slot j * 256 + s. `legendre`: zero at every degree below the order of its slot. `coefficients`: zero at every degree below the order of its slot.
All inputs are finite; a program needn't handle non-finite values.
Results may differ from the reference program's by a relative error of at most 0.025.
Values may be sent and summed in bfloat16 or wider, within the bound.
No kernel may reach another device: no remote copies, remote signals or barrier semaphores. Data moves between devices by JAX's collectives and lax.ppermute only.
A program may use at most 128 MiB of HBM per device.

```python
import math
import jax
import jax.numpy as jnp
from jax import lax

M = 2048
L = 2048
NLON = 4096
F = 64
NLAT = 256
SLOTS = 256
N_DEG = 16


def order_layout(key):
    paired = jax.random.permutation(jax.random.fold_in(key, 5), M // 2).astype(jnp.int32)
    paired = paired.reshape(M // SLOTS, SLOTS // 2)
    return jnp.concatenate([paired, M - 1 - paired], axis=1).reshape(M)


def draw_order_table(key, part):
    return order_layout(key)


def draw_legendre(key, part):
    orders = order_layout(key)
    degree = lax.iota(jnp.int32, L)
    values = jax.random.normal(jax.random.fold_in(key, 11), (M, L, NLAT), jnp.float32) * (1.0 / math.sqrt(L))
    live = degree[None, :, None] >= orders[:, None, None]
    return jnp.where(live, values, 0.0).astype(jnp.bfloat16)


def draw_coefficients(key, part):
    orders = order_layout(key)
    degree = lax.iota(jnp.int32, L)
    values = jax.random.normal(jax.random.fold_in(key, 17), (M, L, 2 * F), jnp.float32) * (1.0 / math.sqrt(2.0 * M))
    live = degree[None, :, None] >= orders[:, None, None]
    return jnp.where(live, values, 0.0).astype(jnp.bfloat16)


def setup_inputs(seed: int = 0) -> dict:
    seeds = jax.random.split(jax.random.key(seed), 4)
    coefficients = draw_coefficients(jax.random.fold_in(seeds[3], 71), 0)
    legendre = draw_legendre(jax.random.fold_in(seeds[3], 71), 0)
    order_table = draw_order_table(jax.random.fold_in(seeds[3], 71), 0)
    return dict(coefficients=coefficients, legendre=legendre, order_table=order_table)


def build_tables(order_table, weight, index, block, nlon, kind):
    fine = 64
    coarse = block // fine
    outer = lax.iota(jnp.int32, coarse) + (index * coarse).astype(jnp.int32)
    inner = lax.iota(jnp.int32, fine)
    factor = 2.0 * math.pi / nlon
    big_angle = ((order_table[:, None] * (outer[None, :] * fine)) % nlon).astype(kind) * factor
    small_angle = ((order_table[:, None] * inner[None, :]) % nlon).astype(kind) * factor
    cos_big = jnp.cos(big_angle)[:, :, None]
    sin_big = jnp.sin(big_angle)[:, :, None]
    cos_small = jnp.cos(small_angle)[:, None, :]
    sin_small = jnp.sin(small_angle)[:, None, :]
    scaled = weight[:, None, None]
    cos_full = scaled * (cos_big * cos_small - sin_big * sin_small)
    sin_full = -(scaled * (sin_big * cos_small + cos_big * sin_small))
    count = order_table.shape[0]
    return cos_full.reshape(count, block), sin_full.reshape(count, block)


def reference(coefficients, legendre, order_table):
    width = L // N_DEG

    def add_block(total, index):
        start = (index * width).astype(jnp.int32)
        values = lax.dynamic_slice_in_dim(legendre, start, width, 1).astype(jnp.float32)
        weights = lax.dynamic_slice_in_dim(coefficients, start, width, 1).astype(jnp.float32)
        partial_sum = jnp.einsum("slt,slc->tsc", values, weights).astype(jnp.bfloat16)
        partial_sum = lax.optimization_barrier(partial_sum)
        return total + partial_sum.astype(jnp.float32), None

    start_total = jnp.zeros((NLAT, M, 2 * F), jnp.float32)
    summed, _ = lax.scan(add_block, start_total, jnp.arange(N_DEG, dtype=jnp.int32))
    rounded = lax.optimization_barrier(summed.astype(jnp.bfloat16))
    spectra = rounded.astype(summed.dtype)
    spec_real = spectra[:, :, :F]
    spec_imag = spectra[:, :, F:]
    weight = jnp.where(order_table == 0, 1.0, 2.0).astype(summed.dtype)
    block = min(1024, NLON)
    count = NLON // block

    def one_block(index):
        cos_full, sin_full = build_tables(order_table, weight, index, block, NLON, summed.dtype)
        cos_table = lax.optimization_barrier(cos_full.astype(jnp.bfloat16)).astype(summed.dtype)
        sin_table = lax.optimization_barrier(sin_full.astype(jnp.bfloat16)).astype(summed.dtype)
        grid = jnp.einsum("kmf,mn->kfn", spec_real, cos_table)
        grid = grid + jnp.einsum("kmf,mn->kfn", spec_imag, sin_table)
        return grid[:, 0::2, :] * grid[:, 1::2, :]

    blocks = lax.map(one_block, jnp.arange(count, dtype=jnp.int32))
    result = jnp.transpose(blocks, (1, 2, 0, 3)).reshape(NLAT, F // 2, NLON)
    return result.astype(jnp.bfloat16)
```

```python
import math

import jax
import jax.numpy as jnp
from jax import lax
from jax.experimental import pallas as pl
from jax.experimental.pallas import tpu as pltpu
from jax.sharding import PartitionSpec as P

NLON = 4096
QUARTER = NLON // 4
WIDE = QUARTER + 256
F32 = jnp.float32
BF16 = jnp.bfloat16


def legendre_kernel(leg_ref, coef_ref, out_ref, turned):
    step = leg_ref.shape[0]
    for s in range(step):
        turned[:, s, :] = lax.dot_general(
            leg_ref[s], coef_ref[s], (((0,), (0,)), ((), ())), preferred_element_type=F32
        )
    out_ref[...] = turned[...].astype(BF16)


def legendre_sums(legendre, coefficients, step=16):
    slots, width, nlat = legendre.shape
    channels = coefficients.shape[2]
    return pl.pallas_call(
        legendre_kernel,
        out_shape=jax.ShapeDtypeStruct((nlat, slots, channels), BF16),
        grid=(slots // step,),
        in_specs=[
            pl.BlockSpec((step, width, nlat), lambda i: (i, 0, 0)),
            pl.BlockSpec((step, width, channels), lambda i: (i, 0, 0)),
        ],
        out_specs=pl.BlockSpec((nlat, step, channels), lambda i: (0, i, 0)),
        scratch_shapes=[pltpu.VMEM((nlat, step, channels), F32)],
        compiler_params=pltpu.CompilerParams(vmem_limit_bytes=40 * 2**20),
        name="legendre_sums",
    )(legendre, coefficients)


def table_kernel(cos_ref, sin_ref, cos_step, sin_step, cos_out, sin_out):
    c = cos_ref[...]
    s = sin_ref[...]
    dc = cos_step[...]
    ds = sin_step[...]
    for q in range(WIDE // 128):
        cos_out[:, pl.ds(128 * q, 128)] = c.astype(BF16)
        sin_out[:, pl.ds(128 * q, 128)] = (-s).astype(BF16)
        if q + 1 < WIDE // 128:
            c, s = c * dc - s * ds, s * dc + c * ds


def build_tables(order_table):
    count = order_table.shape[0]
    factor = 2.0 * math.pi / NLON
    weight = jnp.where(order_table == 0, 1.0, 2.0).astype(F32)[:, None]
    inner = lax.iota(jnp.int32, 128)
    small = (order_table[:, None] * inner[None, :] % NLON).astype(F32) * factor
    big = (order_table * 128 % NLON).astype(F32) * factor
    cos_big = jnp.broadcast_to(jnp.cos(big)[:, None], (count, 128))
    sin_big = jnp.broadcast_to(jnp.sin(big)[:, None], (count, 128))
    rows = 256
    narrow = pl.BlockSpec((rows, 128), lambda i: (i, 0))
    wide = pl.BlockSpec((rows, WIDE), lambda i: (i, 0))
    return pl.pallas_call(
        table_kernel,
        out_shape=[jax.ShapeDtypeStruct((count, WIDE), BF16)] * 2,
        grid=(count // rows,),
        in_specs=[narrow] * 4,
        out_specs=[wide] * 2,
        compiler_params=pltpu.CompilerParams(vmem_limit_bytes=40 * 2**20),
        name="build_tables",
    )(weight * jnp.cos(small), weight * jnp.sin(small), cos_big, sin_big)


def fourier_kernel(spec_ref, even_ref, pick_ref, turn_ref, cos_ref, sin_ref, out_ref,
                   left_cos, left_sin, plus, minus):
    blocks, lats, slots, channels = spec_ref.shape
    quart = channels // 4
    half = 2 * lats * quart
    step = pl.program_id(0)
    nsteps = pl.num_programs(0)

    @pl.when(step == 0)
    def _():
        for j in range(blocks):
            cols = pl.ds(j * slots, slots)
            even = even_ref[pl.ds(0, 1), cols]
            for k in range(lats):
                turned = lax.dot_general(
                    pick_ref[...], spec_ref[j, k], (((1,), (1,)), ((), ())),
                    preferred_element_type=F32,
                )
                evens = turned * even
                odds = turned - evens
                for o, part in enumerate((evens, odds)):
                    part = part.astype(BF16)
                    for h in range(2):
                        rows = pl.ds(o * half + (h * lats + k) * quart, quart)
                        left_cos[rows, cols] = part[h * quart:(h + 1) * quart]
                        left_sin[rows, cols] = part[(2 + h) * quart:(3 + h) * quart]

    cosines = jnp.dot(left_cos[...], cos_ref[...], preferred_element_type=F32)
    sines = jnp.dot(left_sin[...], sin_ref[...], preferred_element_type=F32)
    cos_sum = cosines[:half] + cosines[half:]
    cos_dif = cosines[:half] - cosines[half:]
    sin_sum = sines[:half] + sines[half:]
    sin_dif = sines[:half] - sines[half:]
    pairs = half // 2
    width = cos_ref.shape[1]
    cols = pl.ds(pl.multiple_of(step * width, width), width)

    def product(grid):
        return (grid[:pairs] * grid[pairs:]).astype(BF16)

    plus[:, cols] = product(cos_sum - sin_sum)
    minus[:, cols] = product(cos_dif - sin_dif)

    @pl.when(step < nsteps - 1)
    def _():
        first = product(cos_sum + sin_sum).reshape(lats, quart, width)
        third = product(cos_dif + sin_dif).reshape(lats, quart, width)
        out_ref[:, :, cols] = first
        out_ref[:, :, pl.ds(pl.multiple_of(2 * QUARTER + step * width, width), width)] = third

    @pl.when(step == nsteps - 1)
    def _():
        for b in range(QUARTER // 128):
            source = pl.ds(QUARTER - 128 - 128 * b, 256)
            for start, held in ((3 * QUARTER, plus), (QUARTER, minus)):
                block = jnp.dot(held[:, source], turn_ref[...], preferred_element_type=F32)
                out_ref[:, :, pl.ds(start + 128 * b, 128)] = block.astype(BF16).reshape(
                    lats, quart, 128
                )


def fourier_products(spectra, order_table, cos_table, sin_table):
    blocks, lats, slots, channels = spectra.shape
    count = order_table.shape[0]
    fields = channels // 2
    even = jnp.where(order_table % 2 == 0, 1.0, 0.0).astype(F32)
    even = jnp.broadcast_to(even[None, :], (8, count))
    c = lax.iota(jnp.int32, channels)
    part, field = c // fields, c % fields
    place = part * fields + (field % 2) * (fields // 2) + field // 2
    pick = (lax.iota(jnp.int32, channels)[:, None] == place[None, :]).astype(BF16)
    turn = (lax.iota(jnp.int32, 256)[:, None] == 128 - lax.iota(jnp.int32, 128)[None, :]).astype(BF16)
    width = 256
    full = lambda shape: pl.BlockSpec(shape, lambda i: (0,) * len(shape))
    half = lats * fields
    return pl.pallas_call(
        fourier_kernel,
        out_shape=jax.ShapeDtypeStruct((lats, fields // 2, NLON), BF16),
        grid=(WIDE // width,),
        in_specs=[
            full(spectra.shape),
            full(even.shape),
            full(pick.shape),
            full(turn.shape),
            pl.BlockSpec((count, width), lambda i: (0, i)),
            pl.BlockSpec((count, width), lambda i: (0, i)),
        ],
        out_specs=full((lats, fields // 2, NLON)),
        scratch_shapes=[
            pltpu.VMEM((2 * half, count), BF16),
            pltpu.VMEM((2 * half, count), BF16),
            pltpu.VMEM((half // 2, WIDE), BF16),
            pltpu.VMEM((half // 2, WIDE), BF16),
        ],
        compiler_params=pltpu.CompilerParams(vmem_limit_bytes=48 * 2**20),
        name="fourier_products",
    )(spectra, even, pick, turn, cos_table, sin_table)


def local(coefficients, legendre, order_table):
    partial = legendre_sums(legendre, coefficients)
    summed = lax.psum_scatter(partial, "deg", scatter_dimension=0, tiled=True)
    cos_table, sin_table = build_tables(order_table)
    rows, slots, channels = summed.shape
    groups = order_table.shape[0] // slots
    sent = summed.reshape(groups, rows // groups, slots, channels)
    spectra = lax.all_to_all(sent, "ord", split_axis=0, concat_axis=0, tiled=True)
    return fourier_products(spectra, order_table, cos_table, sin_table)


def solution(mesh):
    placed = (P("ord", "deg", None), P("ord", "deg", None), P())
    return jax.shard_map(
        local, mesh=mesh, in_specs=placed, out_specs=P(("deg", "ord"), None, None), check_vma=False
    )
```

```python
import functools
import math

import jax
import jax.numpy as jnp
from jax import lax
from jax.experimental import pallas as pl
from jax.experimental.pallas import tpu as pltpu
from jax.sharding import PartitionSpec as P

NLON = 4096
QUARTER = NLON // 4
WIDE = QUARTER + 256
F32 = jnp.float32
BF16 = jnp.bfloat16


CHUNKS = 2
SIDE = 4


def legendre_kernel(place_ref, leg_ref, coef_ref, _, first_ref, second_ref, third_ref, one_ref,
                    own_ref, turned, *, strides):
    step = leg_ref.shape[0]
    rows = turned.shape[0] // (SIDE * SIDE)
    sums = [
        lax.dot_general(
            leg_ref[s], coef_ref[s], (((0,), (0,)), ((), ())), preferred_element_type=F32
        ).astype(BF16)
        for s in range(step)
    ]
    turned[...] = jnp.swapaxes(jnp.stack(sums, axis=0), 0, 1)
    here = (place_ref[0], place_ref[1])
    half = SIDE // 2
    parts = (
        (first_ref, [(1, r) for r in range(half)] + [(2, r) for r in range(half)]),
        (second_ref, [(3, r) for r in range(half, SIDE)] + [(2, r) for r in range(half, SIDE)]),
        (third_ref, [(3, r) for r in range(half)]),
        (one_ref, [(1, r) for r in range(half, SIDE)]),
        (own_ref, [(0, r) for r in range(SIDE)]),
    )
    for ref, blocks in parts:
        for i, (r1, r2) in enumerate(blocks):
            block = (here[0] ^ r1) * strides[0] + (here[1] ^ r2) * strides[1]
            source = pl.ds(pl.multiple_of(block * rows, rows), rows)
            ref[i] = turned[source]


def legendre_sums(place, legendre, coefficients, after, start, slots, strides, step=16):
    width, nlat = legendre.shape[1:]
    channels = coefficients.shape[2]
    rows = nlat // (SIDE * SIDE)
    offset = start // step
    counts = (4, 4, 2, 2, 4)
    return pl.pallas_call(
        functools.partial(legendre_kernel, strides=strides),
        out_shape=[jax.ShapeDtypeStruct((n, rows, slots, channels), BF16) for n in counts],
        grid=(slots // step,),
        in_specs=[
            pl.BlockSpec(memory_space=pltpu.SMEM),
            pl.BlockSpec((step, width, nlat), lambda i: (i + offset, 0, 0)),
            pl.BlockSpec((step, width, channels), lambda i: (i + offset, 0, 0)),
            pl.BlockSpec(memory_space=pl.ANY),
        ],
        out_specs=[pl.BlockSpec((n, rows, step, channels), lambda i: (0, 0, i, 0)) for n in counts],
        scratch_shapes=[pltpu.VMEM((nlat, step, channels), BF16)],
        compiler_params=pltpu.CompilerParams(vmem_limit_bytes=40 * 2**20),
        name="legendre_sums",
    )(place, legendre, coefficients, after)


def add(*parts):
    total = parts[0].astype(F32)
    for part in parts[1:]:
        total = total + part.astype(F32)
    return total.astype(BF16)


def pass_kernel(got_first, got_second, third, one, first_out, second_out):
    half = third.shape[0]
    first_out[...] = add(third[...], got_first[half:])
    second_out[...] = add(one[...], got_second[half:])


def turn_kernel(*refs):
    outs = refs[-5:]
    first_out, second_out, third_out, one_out, own_out = outs
    for c in range(CHUNKS):
        got_first, got_second, last_first, last_second, own = refs[5 * c:5 * c + 5]
        half = got_first.shape[0] // 2
        rows, slots = own.shape[1] // 2, own.shape[2]
        cols = pl.ds(c * slots, slots)

        def sums(block, part):
            if block < half:
                got, last, at = got_first, last_first, block
            else:
                got, last, at = got_second, last_second, block - half
            return add(own[block, part], got[at, part], last[at, part])

        low, high = pl.ds(0, rows), pl.ds(rows, rows)
        first_out[0:rows, cols] = sums(1, low)
        first_out[rows:, cols] = sums(2, low)
        second_out[0:rows, cols] = sums(3, high)
        second_out[rows:, cols] = sums(2, high)
        third_out[:, cols] = sums(3, low)
        one_out[:, cols] = sums(1, high)
        own_out[0:rows, cols] = sums(0, low)
        own_out[rows:, cols] = sums(0, high)


def join_kernel(*refs):
    out = refs[-1]
    count = (len(refs) - 1) // 5
    slots = out.shape[1] // count
    rows = out.shape[0] // 2
    for i in range(count):
        got_first, got_second, last_first, last_second, own = refs[5 * i:5 * i + 5]
        cols = pl.ds(i * slots, slots)
        out[0:rows, cols] = add(own[0:rows], got_first[0:rows], last_first[...])
        out[rows:, cols] = add(own[rows:], got_second[0:rows], last_second[...])


def call(kernel, name, shapes, after, *arrays):
    return pl.pallas_call(
        lambda _, *refs: kernel(*refs),
        out_shape=[jax.ShapeDtypeStruct(s, BF16) for s in shapes],
        in_specs=[pl.BlockSpec(memory_space=pl.ANY)]
        + [pl.BlockSpec(memory_space=pltpu.VMEM)] * len(arrays),
        compiler_params=pltpu.CompilerParams(vmem_limit_bytes=40 * 2**20),
        name=name,
    )(after, *arrays)


def exchange(array, bits):
    return lax.ppermute(array, "deg", [(d, d ^ bits) for d in range(SIDE * SIDE)])


def start_sums(parts, unit):
    first, second, third, one, own = parts
    return exchange(first, unit), exchange(second, 3 * unit), third, one, own


def pass_sums(state, unit, after):
    got_first, got_second, third, one, own = state
    send_first, send_second = call(
        pass_kernel, "pass_sums", (third.shape, one.shape), after, got_first, got_second, third, one
    )
    last_first = exchange(send_first, 3 * unit)
    last_second = exchange(send_second, unit)
    return (got_first, got_second, last_first, last_second, own), send_second


def turn_sums(states, unit, after):
    rows, slots, channels = states[0][-1].shape[1:]
    slots = slots * CHUNKS
    whole, half = (rows, slots, channels), (rows // 2, slots, channels)
    arrays = [a for state in states for a in state]
    parts = call(turn_kernel, "turn_sums", (whole, whole, half, half, whole), after, *arrays)
    return start_sums(parts, unit), parts[3]


def table_kernel(_, cos_ref, sin_ref, cos_step, sin_step, cos_out, sin_out):
    c = cos_ref[...]
    s = sin_ref[...]
    dc = cos_step[...]
    ds = sin_step[...]
    for q in range(WIDE // 128):
        cos_out[:, pl.ds(128 * q, 128)] = c.astype(BF16)
        sin_out[:, pl.ds(128 * q, 128)] = (-s).astype(BF16)
        if q + 1 < WIDE // 128:
            c, s = c * dc - s * ds, s * dc + c * ds


def build_tables(order_table, after):
    count = order_table.shape[0]
    factor = 2.0 * math.pi / NLON
    weight = jnp.where(order_table == 0, 1.0, 2.0).astype(F32)[:, None]
    inner = lax.iota(jnp.int32, 128)
    small = (order_table[:, None] * inner[None, :] % NLON).astype(F32) * factor
    big = (order_table * 128 % NLON).astype(F32) * factor
    cos_big = jnp.broadcast_to(jnp.cos(big)[:, None], (count, 128))
    sin_big = jnp.broadcast_to(jnp.sin(big)[:, None], (count, 128))
    rows = 256
    narrow = pl.BlockSpec((rows, 128), lambda i: (i, 0))
    wide = pl.BlockSpec((rows, WIDE), lambda i: (i, 0))
    return pl.pallas_call(
        table_kernel,
        out_shape=[pltpu.HBM((count, WIDE), BF16)] * 2,
        grid=(count // rows,),
        in_specs=[pl.BlockSpec(memory_space=pl.ANY)] + [narrow] * 4,
        out_specs=[wide] * 2,
        compiler_params=pltpu.CompilerParams(vmem_limit_bytes=40 * 2**20),
        name="build_tables",
    )(after, weight * jnp.cos(small), weight * jnp.sin(small), cos_big, sin_big)


def fourier_kernel(spec_ref, even_ref, pick_ref, turn_ref, cos_ref, sin_ref, out_ref,
                   left_cos, left_sin, plus, minus):
    blocks, lats, slots, channels = spec_ref.shape
    quart = channels // 4
    half = 2 * lats * quart
    step = pl.program_id(0)
    nsteps = pl.num_programs(0)

    @pl.when(step == 0)
    def _():
        for j in range(blocks):
            cols = pl.ds(j * slots, slots)
            even = even_ref[pl.ds(0, 1), cols]
            for k in range(lats):
                turned = lax.dot_general(
                    pick_ref[...], spec_ref[j, k], (((1,), (1,)), ((), ())),
                    preferred_element_type=F32,
                )
                evens = turned * even
                odds = turned - evens
                for o, part in enumerate((evens, odds)):
                    part = part.astype(BF16)
                    for h in range(2):
                        rows = pl.ds(o * half + (h * lats + k) * quart, quart)
                        left_cos[rows, cols] = part[h * quart:(h + 1) * quart]
                        left_sin[rows, cols] = part[(2 + h) * quart:(3 + h) * quart]

    cosines = jnp.dot(left_cos[...], cos_ref[...], preferred_element_type=F32)
    sines = jnp.dot(left_sin[...], sin_ref[...], preferred_element_type=F32)
    cos_sum = cosines[:half] + cosines[half:]
    cos_dif = cosines[:half] - cosines[half:]
    sin_sum = sines[:half] + sines[half:]
    sin_dif = sines[:half] - sines[half:]
    pairs = half // 2
    width = cos_ref.shape[1]
    cols = pl.ds(pl.multiple_of(step * width, width), width)

    def product(grid):
        return (grid[:pairs] * grid[pairs:]).astype(BF16)

    plus[:, cols] = product(cos_sum - sin_sum)
    minus[:, cols] = product(cos_dif - sin_dif)

    @pl.when(step < nsteps - 1)
    def _():
        first = product(cos_sum + sin_sum).reshape(lats, quart, width)
        third = product(cos_dif + sin_dif).reshape(lats, quart, width)
        out_ref[:, :, cols] = first
        out_ref[:, :, pl.ds(pl.multiple_of(2 * QUARTER + step * width, width), width)] = third

    @pl.when(step == nsteps - 1)
    def _():
        for b in range(QUARTER // 128):
            source = pl.ds(QUARTER - 128 - 128 * b, 256)
            for start, held in ((3 * QUARTER, plus), (QUARTER, minus)):
                block = jnp.dot(held[:, source], turn_ref[...], preferred_element_type=F32)
                out_ref[:, :, pl.ds(start + 128 * b, 128)] = block.astype(BF16).reshape(
                    lats, quart, 128
                )


def fourier_products(spectra, order_table, cos_table, sin_table):
    blocks, lats, slots, channels = spectra.shape
    count = order_table.shape[0]
    fields = channels // 2
    even = jnp.where(order_table % 2 == 0, 1.0, 0.0).astype(F32)
    even = jnp.broadcast_to(even[None, :], (8, count))
    c = lax.iota(jnp.int32, channels)
    part, field = c // fields, c % fields
    place = part * fields + (field % 2) * (fields // 2) + field // 2
    pick = (lax.iota(jnp.int32, channels)[:, None] == place[None, :]).astype(BF16)
    turn = (lax.iota(jnp.int32, 256)[:, None] == 128 - lax.iota(jnp.int32, 128)[None, :]).astype(BF16)
    width = 256
    full = lambda shape: pl.BlockSpec(shape, lambda i: (0,) * len(shape))
    half = lats * fields
    return pl.pallas_call(
        fourier_kernel,
        out_shape=jax.ShapeDtypeStruct((lats, fields // 2, NLON), BF16),
        grid=(WIDE // width,),
        in_specs=[
            full(spectra.shape),
            full(even.shape),
            full(pick.shape),
            full(turn.shape),
            pl.BlockSpec((count, width), lambda i: (0, i)),
            pl.BlockSpec((count, width), lambda i: (0, i)),
        ],
        out_specs=full((lats, fields // 2, NLON)),
        scratch_shapes=[
            pltpu.VMEM((2 * half, count), BF16),
            pltpu.VMEM((2 * half, count), BF16),
            pltpu.VMEM((half // 2, WIDE), BF16),
            pltpu.VMEM((half // 2, WIDE), BF16),
        ],
        compiler_params=pltpu.CompilerParams(vmem_limit_bytes=40 * 2**20),
        name="fourier_products",
    )(spectra, even, pick, turn, cos_table, sin_table)


def local(coefficients, legendre, order_table):
    here = lax.axis_index("deg")
    y, x = here // SIDE, here % SIDE
    total, channels = coefficients.shape[0], coefficients.shape[2]
    groups = order_table.shape[0] // total
    slots = total // (2 * CHUNKS)
    coefficients = pltpu.with_memory_space_constraint(coefficients, pltpu.HBM)
    legendre = pltpu.with_memory_space_constraint(legendre, pltpu.HBM)
    units = ((1, SIDE), (SIDE, 1))
    state = {}
    after = order_table
    keys = [(k, way) for k in range(CHUNKS) for way in range(2)]
    for k, way in keys:
        place = jnp.stack([x, y] if way == 0 else [y, x]).astype(jnp.int32)
        parts = legendre_sums(
            place, legendre, coefficients, after, (way * CHUNKS + k) * slots, slots, units[way]
        )
        after = parts[3]
        state[k, way] = start_sums(parts, units[way][0])
    tables = build_tables(order_table, after)
    tables = [pltpu.with_memory_space_constraint(t, pltpu.HBM) for t in tables]
    after = tables[0]
    for k, way in keys:
        state[k, way], after = pass_sums(state[k, way], units[way][0], after)
    ends = []
    for way in range(2):
        end, after = turn_sums([state[k, way] for k in range(CHUNKS)], units[way][1], after)
        ends.append(end)
    for way in range(2):
        ends[way], after = pass_sums(ends[way], units[way][1], after)
    pair = ends[0] + ends[1]
    rows = pair[-1].shape[0]
    (summed,) = call(join_kernel, "join_sums", ((rows, total, channels),), after, *pair)
    sent = summed.reshape(groups, rows // groups, total, channels)
    spectra = lax.all_to_all(sent, "ord", split_axis=0, concat_axis=0, tiled=True)
    return fourier_products(spectra, order_table, *tables)


def solution(mesh):
    placed = (P("ord", "deg", None), P("ord", "deg", None), P())
    return jax.shard_map(
        local, mesh=mesh, in_specs=placed, out_specs=P(("deg", "ord"), None, None), check_vma=False
    )
```

```python
import functools
import math

import jax
import jax.numpy as jnp
from jax import lax
from jax.experimental import pallas as pl
from jax.experimental.pallas import tpu as pltpu
from jax.sharding import PartitionSpec as P

NLON = 4096
QUARTER = NLON // 4
WIDE = QUARTER + 256
F32 = jnp.float32
BF16 = jnp.bfloat16


CHUNKS = (48, 80)
SIDE = 4


def legendre_kernel(place_ref, leg_ref, coef_ref, _, first_ref, second_ref, third_ref, one_ref,
                    own_ref, turned, *, strides):
    step = leg_ref.shape[0]
    rows = turned.shape[0] // (SIDE * SIDE)
    sums = [
        lax.dot_general(
            leg_ref[s], coef_ref[s], (((0,), (0,)), ((), ())), preferred_element_type=F32
        ).astype(BF16)
        for s in range(step)
    ]
    turned[...] = jnp.swapaxes(jnp.stack(sums, axis=0), 0, 1)
    here = (place_ref[0], place_ref[1])
    half = SIDE // 2
    parts = (
        (first_ref, [(1, r) for r in range(half)] + [(2, r) for r in range(half)]),
        (second_ref, [(3, r) for r in range(half, SIDE)] + [(2, r) for r in range(half, SIDE)]),
        (third_ref, [(3, r) for r in range(half)]),
        (one_ref, [(1, r) for r in range(half, SIDE)]),
        (own_ref, [(0, r) for r in range(SIDE)]),
    )
    for ref, blocks in parts:
        for i, (r1, r2) in enumerate(blocks):
            block = (here[0] ^ r1) * strides[0] + (here[1] ^ r2) * strides[1]
            source = pl.ds(pl.multiple_of(block * rows, rows), rows)
            ref[i] = turned[source]


def legendre_sums(place, legendre, coefficients, after, start, slots, strides, step=16):
    width, nlat = legendre.shape[1:]
    channels = coefficients.shape[2]
    rows = nlat // (SIDE * SIDE)
    offset = start // step
    counts = (4, 4, 2, 2, 4)
    return pl.pallas_call(
        functools.partial(legendre_kernel, strides=strides),
        out_shape=[jax.ShapeDtypeStruct((n, rows, slots, channels), BF16) for n in counts],
        grid=(slots // step,),
        in_specs=[
            pl.BlockSpec(memory_space=pltpu.SMEM),
            pl.BlockSpec((step, width, nlat), lambda i: (i + offset, 0, 0)),
            pl.BlockSpec((step, width, channels), lambda i: (i + offset, 0, 0)),
            pl.BlockSpec(memory_space=pl.ANY),
        ],
        out_specs=[pl.BlockSpec((n, rows, step, channels), lambda i: (0, 0, i, 0)) for n in counts],
        scratch_shapes=[pltpu.VMEM((nlat, step, channels), BF16)],
        compiler_params=pltpu.CompilerParams(vmem_limit_bytes=40 * 2**20),
        name="legendre_sums",
    )(place, legendre, coefficients, after)


def add(*parts):
    total = parts[0].astype(F32)
    for part in parts[1:]:
        total = total + part.astype(F32)
    return total.astype(BF16)


def pass_kernel(got_first, got_second, third, one, first_out, second_out):
    half = third.shape[0]
    first_out[...] = add(third[...], got_first[half:])
    second_out[...] = add(one[...], got_second[half:])


def turn_kernel(*refs):
    outs = refs[-SIDE:]
    start = 0
    for c in range(len(CHUNKS)):
        got_first, got_second, last_first, last_second, own = refs[5 * c:5 * c + 5]
        half = SIDE // 2
        slots = own.shape[2]
        cols = pl.ds(start, slots)
        start += slots
        for block in range(SIDE):
            if block < half:
                got, last, at = got_first, last_first, block
            else:
                got, last, at = got_second, last_second, block - half
            outs[block][:, cols] = add(own[block], got[at], last[at])


def join_kernel(*refs):
    out = refs[-1]
    count = (len(refs) - 1) // SIDE
    slots = out.shape[1] // count
    for i in range(count):
        cols = pl.ds(i * slots, slots)
        out[:, cols] = add(*[ref[...] for ref in refs[SIDE * i:SIDE * i + SIDE]])


def call(kernel, name, shapes, after, *arrays):
    return pl.pallas_call(
        lambda _, *refs: kernel(*refs),
        out_shape=[jax.ShapeDtypeStruct(s, BF16) for s in shapes],
        in_specs=[pl.BlockSpec(memory_space=pl.ANY)]
        + [pl.BlockSpec(memory_space=pltpu.VMEM)] * len(arrays),
        compiler_params=pltpu.CompilerParams(vmem_limit_bytes=40 * 2**20),
        name=name,
    )(after, *arrays)


def exchange(array, bits):
    return lax.ppermute(array, "deg", [(d, d ^ bits) for d in range(SIDE * SIDE)])


def later(array, *before):
    return lax.optimization_barrier((array, *before))[0]


def start_sums(parts, unit, before=((), ())):
    first, second, third, one, own = parts
    return (
        exchange(later(first, *before[0]), unit),
        exchange(later(second, *before[1]), 3 * unit),
        third, one, own,
    )


def pass_sums(state, unit, after, before=((), ())):
    got_first, got_second, third, one, own = state
    send_first, send_second = call(
        pass_kernel, "pass_sums", (third.shape, one.shape), after, got_first, got_second, third, one
    )
    last_first = exchange(later(send_first, *before[1]), 3 * unit)
    last_second = exchange(later(send_second, *before[0]), unit)
    return (got_first, got_second, last_first, last_second, own), send_second


def turn_sums(states, unit, after):
    rows, _, channels = states[0][-1].shape[1:]
    slots = sum(state[-1].shape[2] for state in states)
    arrays = [a for state in states for a in state]
    own, one, two, three = call(
        turn_kernel, "turn_sums", ((rows, slots, channels),) * SIDE, after, *arrays
    )
    return (own, exchange(one, unit), exchange(three, 3 * unit), exchange(two, 2 * unit)), own


def table_kernel(_, cos_ref, sin_ref, cos_step, sin_step, cos_out, sin_out):
    c = cos_ref[...]
    s = sin_ref[...]
    dc = cos_step[...]
    ds = sin_step[...]
    for q in range(WIDE // 128):
        cos_out[:, pl.ds(128 * q, 128)] = c.astype(BF16)
        sin_out[:, pl.ds(128 * q, 128)] = (-s).astype(BF16)
        if q + 1 < WIDE // 128:
            c, s = c * dc - s * ds, s * dc + c * ds


def build_tables(order_table, after):
    count = order_table.shape[0]
    factor = 2.0 * math.pi / NLON
    weight = jnp.where(order_table == 0, 1.0, 2.0).astype(F32)[:, None]
    inner = lax.iota(jnp.int32, 128)
    small = (order_table[:, None] * inner[None, :] % NLON).astype(F32) * factor
    big = (order_table * 128 % NLON).astype(F32) * factor
    cos_big = jnp.broadcast_to(jnp.cos(big)[:, None], (count, 128))
    sin_big = jnp.broadcast_to(jnp.sin(big)[:, None], (count, 128))
    rows = 256
    narrow = pl.BlockSpec((rows, 128), lambda i: (i, 0))
    wide = pl.BlockSpec((rows, WIDE), lambda i: (i, 0))
    return pl.pallas_call(
        table_kernel,
        out_shape=[pltpu.HBM((count, WIDE), BF16)] * 2,
        grid=(count // rows,),
        in_specs=[pl.BlockSpec(memory_space=pl.ANY)] + [narrow] * 4,
        out_specs=[wide] * 2,
        compiler_params=pltpu.CompilerParams(vmem_limit_bytes=40 * 2**20),
        name="build_tables",
    )(after, weight * jnp.cos(small), weight * jnp.sin(small), cos_big, sin_big)


def fourier_kernel(spec_ref, even_ref, pick_ref, turn_ref, cos_ref, sin_ref, out_ref,
                   left_cos, left_sin, plus, minus):
    blocks, lats, slots, channels = spec_ref.shape
    quart = channels // 4
    half = 2 * lats * quart
    step = pl.program_id(0)
    nsteps = pl.num_programs(0)

    @pl.when(step == 0)
    def _():
        for j in range(blocks):
            cols = pl.ds(j * slots, slots)
            even = even_ref[pl.ds(0, 1), cols]
            for k in range(lats):
                turned = lax.dot_general(
                    pick_ref[...], spec_ref[j, k], (((1,), (1,)), ((), ())),
                    preferred_element_type=F32,
                )
                evens = turned * even
                odds = turned - evens
                for o, part in enumerate((evens, odds)):
                    part = part.astype(BF16)
                    for h in range(2):
                        rows = pl.ds(o * half + (h * lats + k) * quart, quart)
                        left_cos[rows, cols] = part[h * quart:(h + 1) * quart]
                        left_sin[rows, cols] = part[(2 + h) * quart:(3 + h) * quart]

    cosines = jnp.dot(left_cos[...], cos_ref[...], preferred_element_type=F32)
    sines = jnp.dot(left_sin[...], sin_ref[...], preferred_element_type=F32)
    cos_sum = cosines[:half] + cosines[half:]
    cos_dif = cosines[:half] - cosines[half:]
    sin_sum = sines[:half] + sines[half:]
    sin_dif = sines[:half] - sines[half:]
    pairs = half // 2
    width = cos_ref.shape[1]
    cols = pl.ds(pl.multiple_of(step * width, width), width)

    def product(grid):
        return (grid[:pairs] * grid[pairs:]).astype(BF16)

    plus[:, cols] = product(cos_sum - sin_sum)
    minus[:, cols] = product(cos_dif - sin_dif)

    @pl.when(step < nsteps - 1)
    def _():
        first = product(cos_sum + sin_sum).reshape(lats, quart, width)
        third = product(cos_dif + sin_dif).reshape(lats, quart, width)
        out_ref[:, :, cols] = first
        out_ref[:, :, pl.ds(pl.multiple_of(2 * QUARTER + step * width, width), width)] = third

    @pl.when(step == nsteps - 1)
    def _():
        for b in range(QUARTER // 128):
            source = pl.ds(QUARTER - 128 - 128 * b, 256)
            for start, held in ((3 * QUARTER, plus), (QUARTER, minus)):
                block = jnp.dot(held[:, source], turn_ref[...], preferred_element_type=F32)
                out_ref[:, :, pl.ds(start + 128 * b, 128)] = block.astype(BF16).reshape(
                    lats, quart, 128
                )


def fourier_products(spectra, order_table, cos_table, sin_table):
    blocks, lats, slots, channels = spectra.shape
    count = order_table.shape[0]
    fields = channels // 2
    even = jnp.where(order_table % 2 == 0, 1.0, 0.0).astype(F32)
    even = jnp.broadcast_to(even[None, :], (8, count))
    c = lax.iota(jnp.int32, channels)
    part, field = c // fields, c % fields
    place = part * fields + (field % 2) * (fields // 2) + field // 2
    pick = (lax.iota(jnp.int32, channels)[:, None] == place[None, :]).astype(BF16)
    turn = (lax.iota(jnp.int32, 256)[:, None] == 128 - lax.iota(jnp.int32, 128)[None, :]).astype(BF16)
    width = 256
    full = lambda shape: pl.BlockSpec(shape, lambda i: (0,) * len(shape))
    half = lats * fields
    return pl.pallas_call(
        fourier_kernel,
        out_shape=jax.ShapeDtypeStruct((lats, fields // 2, NLON), BF16),
        grid=(WIDE // width,),
        in_specs=[
            full(spectra.shape),
            full(even.shape),
            full(pick.shape),
            full(turn.shape),
            pl.BlockSpec((count, width), lambda i: (0, i)),
            pl.BlockSpec((count, width), lambda i: (0, i)),
        ],
        out_specs=full((lats, fields // 2, NLON)),
        scratch_shapes=[
            pltpu.VMEM((2 * half, count), BF16),
            pltpu.VMEM((2 * half, count), BF16),
            pltpu.VMEM((half // 2, WIDE), BF16),
            pltpu.VMEM((half // 2, WIDE), BF16),
        ],
        compiler_params=pltpu.CompilerParams(vmem_limit_bytes=40 * 2**20),
        name="fourier_products",
    )(spectra, even, pick, turn, cos_table, sin_table)


def local(coefficients, legendre, order_table):
    here = lax.axis_index("deg")
    y, x = here // SIDE, here % SIDE
    total, channels = coefficients.shape[0], coefficients.shape[2]
    groups = order_table.shape[0] // total
    coefficients = pltpu.with_memory_space_constraint(coefficients, pltpu.HBM)
    legendre = pltpu.with_memory_space_constraint(legendre, pltpu.HBM)
    units = ((1, SIDE), (SIDE, 1))
    state = {}
    after = legendre
    keys = [(k, way) for k in range(len(CHUNKS)) for way in range(2)]
    parts = {}
    for k, way in keys:
        place = jnp.stack([x, y] if way == 0 else [y, x]).astype(jnp.int32)
        start = way * sum(CHUNKS) + sum(CHUNKS[:k])
        parts[k, way] = legendre_sums(
            place, legendre, coefficients, after, start, CHUNKS[k], units[way]
        )
        after = parts[k, way][3]
    for k, way in keys:
        before = ((), ())
        if k:
            got = state[k - 1, way]
            before = ((got[0], after), (got[1], after))
        state[k, way] = start_sums(parts[k, way], units[way][0], before)
    tables = build_tables(order_table, after)
    tables = [pltpu.with_memory_space_constraint(t, pltpu.HBM) for t in tables]
    after = tables[0]
    for k, way in keys:
        if k:
            got = state[k - 1, way]
            before = ((got[3],), (got[2],))
        else:
            got = state[k + 1, way]
            before = ((got[0],), (got[1],))
        state[k, way], after = pass_sums(state[k, way], units[way][0], after, before)
    ends = []
    for way in range(2):
        end, after = turn_sums([state[k, way] for k in range(len(CHUNKS))], units[way][1], after)
        ends.append(end)
    pair = ends[0] + ends[1]
    rows = pair[0].shape[0]
    (summed,) = call(join_kernel, "join_sums", ((rows, total, channels),), after, *pair)
    sent = summed.reshape(groups, rows // groups, total, channels)
    spectra = lax.all_to_all(sent, "ord", split_axis=0, concat_axis=0, tiled=True)
    return fourier_products(spectra, order_table, *tables)


def solution(mesh):
    placed = (P("ord", "deg", None), P("ord", "deg", None), P())
    return jax.shard_map(
        local, mesh=mesh, in_specs=placed, out_specs=P(("deg", "ord"), None, None), check_vma=False
    )
```

```python
import functools
import math

import jax
import jax.numpy as jnp
from jax import lax
from jax.experimental import pallas as pl
from jax.experimental.pallas import tpu as pltpu
from jax.sharding import PartitionSpec as P

NLON = 4096
QUARTER = NLON // 4
BLOCK = 256
WIDE = QUARTER + BLOCK
F32 = jnp.float32
BF16 = jnp.bfloat16


CHUNKS = (48, 80)
SIDE = 4


def legendre_kernel(place_ref, leg_ref, coef_ref, _, first_ref, second_ref, third_ref, one_ref,
                    own_ref, turned, *, strides):
    step = leg_ref.shape[0]
    rows = turned.shape[0] // (SIDE * SIDE)
    sums = [
        lax.dot_general(
            leg_ref[s], coef_ref[s], (((0,), (0,)), ((), ())), preferred_element_type=F32
        ).astype(BF16)
        for s in range(step)
    ]
    turned[...] = jnp.swapaxes(jnp.stack(sums, axis=0), 0, 1)
    here = (place_ref[0], place_ref[1])
    half = SIDE // 2
    parts = (
        (first_ref, [(1, r) for r in range(half)] + [(2, r) for r in range(half)]),
        (second_ref, [(3, r) for r in range(half, SIDE)] + [(2, r) for r in range(half, SIDE)]),
        (third_ref, [(3, r) for r in range(half)]),
        (one_ref, [(1, r) for r in range(half, SIDE)]),
        (own_ref, [(0, r) for r in range(SIDE)]),
    )
    for ref, blocks in parts:
        for i, (r1, r2) in enumerate(blocks):
            block = (here[0] ^ r1) * strides[0] + (here[1] ^ r2) * strides[1]
            source = pl.ds(pl.multiple_of(block * rows, rows), rows)
            ref[i] = turned[source]


def legendre_sums(place, legendre, coefficients, after, start, slots, strides, step=16):
    width, nlat = legendre.shape[1:]
    channels = coefficients.shape[2]
    rows = nlat // (SIDE * SIDE)
    offset = start // step
    counts = (4, 4, 2, 2, 4)
    return pl.pallas_call(
        functools.partial(legendre_kernel, strides=strides),
        out_shape=[jax.ShapeDtypeStruct((n, rows, slots, channels), BF16) for n in counts],
        grid=(slots // step,),
        in_specs=[
            pl.BlockSpec(memory_space=pltpu.SMEM),
            pl.BlockSpec((step, width, nlat), lambda i: (i + offset, 0, 0)),
            pl.BlockSpec((step, width, channels), lambda i: (i + offset, 0, 0)),
            pl.BlockSpec(memory_space=pl.ANY),
        ],
        out_specs=[pl.BlockSpec((n, rows, step, channels), lambda i: (0, 0, i, 0)) for n in counts],
        scratch_shapes=[pltpu.VMEM((nlat, step, channels), BF16)],
        compiler_params=pltpu.CompilerParams(vmem_limit_bytes=40 * 2**20),
        name="legendre_sums",
    )(place, legendre, coefficients, after)


def add(*parts):
    total = parts[0].astype(F32)
    for part in parts[1:]:
        total = total + part.astype(F32)
    return total.astype(BF16)


def pass_kernel(got_first, got_second, third, one, first_out, second_out):
    half = third.shape[0]
    first_out[...] = add(third[...], got_first[half:])
    second_out[...] = add(one[...], got_second[half:])


def turn_kernel(*refs):
    outs = refs[-SIDE:]
    start = 0
    for c in range(len(CHUNKS)):
        got_first, got_second, last_first, last_second, own = refs[5 * c:5 * c + 5]
        half = SIDE // 2
        slots = own.shape[2]
        cols = pl.ds(start, slots)
        start += slots
        for block in range(SIDE):
            if block < half:
                got, last, at = got_first, last_first, block
            else:
                got, last, at = got_second, last_second, block - half
            outs[block][:, cols] = add(own[block], got[at], last[at])


def halve_kernel(*refs):
    outs = refs[-5:]
    first_out, second_out, third_out, one_out, own_out = outs
    start = 0
    for c in range(len(CHUNKS)):
        got_first, got_second, last_first, last_second, own = refs[5 * c:5 * c + 5]
        half = got_first.shape[0] // 2
        rows, slots = own.shape[1] // 2, own.shape[2]
        cols = pl.ds(start, slots)
        start += slots

        def sums(block, part):
            if block < half:
                got, last, at = got_first, last_first, block
            else:
                got, last, at = got_second, last_second, block - half
            return add(own[block, part], got[at, part], last[at, part])

        low, high = pl.ds(0, rows), pl.ds(rows, rows)
        first_out[0:rows, cols] = sums(1, low)
        first_out[rows:, cols] = sums(2, low)
        second_out[0:rows, cols] = sums(3, high)
        second_out[rows:, cols] = sums(2, high)
        third_out[:, cols] = sums(3, low)
        one_out[:, cols] = sums(1, high)
        own_out[0:rows, cols] = sums(0, low)
        own_out[rows:, cols] = sums(0, high)


def join_kernel(*refs):
    out = refs[-1]
    slots = out.shape[1] // 2
    rows = out.shape[0] // 2
    out[:, 0:slots] = add(*[ref[...] for ref in refs[:SIDE]])
    got_first, got_second, last_first, last_second, own = refs[SIDE:-1]
    cols = pl.ds(slots, slots)
    out[0:rows, cols] = add(own[0:rows], got_first[0:rows], last_first[...])
    out[rows:, cols] = add(own[rows:], got_second[0:rows], last_second[...])


def call(kernel, name, shapes, after, *arrays):
    return pl.pallas_call(
        lambda _, *refs: kernel(*refs),
        out_shape=[jax.ShapeDtypeStruct(s, BF16) for s in shapes],
        in_specs=[pl.BlockSpec(memory_space=pl.ANY)]
        + [pl.BlockSpec(memory_space=pltpu.VMEM)] * len(arrays),
        compiler_params=pltpu.CompilerParams(vmem_limit_bytes=40 * 2**20),
        name=name,
    )(after, *arrays)


def exchange(array, bits):
    return lax.ppermute(array, "deg", [(d, d ^ bits) for d in range(SIDE * SIDE)])


def later(array, *before):
    return lax.optimization_barrier((array, *before))[0]


def start_sums(parts, unit, before=((), ())):
    first, second, third, one, own = parts
    return (
        exchange(later(first, *before[0]), unit),
        exchange(later(second, *before[1]), 3 * unit),
        third, one, own,
    )


def pass_sums(state, unit, after, before=((), ())):
    got_first, got_second, third, one, own = state
    send_first, send_second = call(
        pass_kernel, "pass_sums", (third.shape, one.shape), after, got_first, got_second, third, one
    )
    last_first = exchange(later(send_first, *before[1]), 3 * unit)
    last_second = exchange(later(send_second, *before[0]), unit)
    return (got_first, got_second, last_first, last_second, own), send_second


def turn_sums(states, unit, after):
    rows, _, channels = states[0][-1].shape[1:]
    slots = sum(state[-1].shape[2] for state in states)
    arrays = [a for state in states for a in state]
    own, one, two, three = call(
        turn_kernel, "turn_sums", ((rows, slots, channels),) * SIDE, after, *arrays
    )
    return (own, exchange(one, unit), exchange(three, 3 * unit), exchange(two, 2 * unit)), own


def halve_sums(states, unit, after):
    rows, _, channels = states[0][-1].shape[1:]
    slots = sum(state[-1].shape[2] for state in states)
    whole, half = (rows, slots, channels), (rows // 2, slots, channels)
    arrays = [a for state in states for a in state]
    parts = call(halve_kernel, "halve_sums", (whole, whole, half, half, whole), after, *arrays)
    return pass_sums(start_sums(parts, unit), unit, parts[3])


def table_kernel(_, cos_ref, sin_ref, cos_step, sin_step, cos_out, sin_out):
    c = cos_ref[...]
    s = sin_ref[...]
    dc = cos_step[...]
    ds = sin_step[...]
    for q in range(WIDE // 128):
        cols = pl.ds(128 * q % BLOCK, 128)
        cos_out[128 * q // BLOCK, :, cols] = c.astype(BF16)
        sin_out[128 * q // BLOCK, :, cols] = (-s).astype(BF16)
        if q + 1 < WIDE // 128:
            c, s = c * dc - s * ds, s * dc + c * ds


def build_tables(order_table, after):
    count = order_table.shape[0]
    factor = 2.0 * math.pi / NLON
    weight = jnp.where(order_table == 0, 1.0, 2.0).astype(F32)[:, None]
    inner = lax.iota(jnp.int32, 128)
    small = (order_table[:, None] * inner[None, :] % NLON).astype(F32) * factor
    big = (order_table * 128 % NLON).astype(F32) * factor
    cos_big = jnp.broadcast_to(jnp.cos(big)[:, None], (count, 128))
    sin_big = jnp.broadcast_to(jnp.sin(big)[:, None], (count, 128))
    rows = 256
    narrow = pl.BlockSpec((rows, 128), lambda i: (i, 0))
    wide = pl.BlockSpec((WIDE // BLOCK, rows, BLOCK), lambda i: (0, i, 0))
    return pl.pallas_call(
        table_kernel,
        out_shape=[pltpu.HBM((WIDE // BLOCK, count, BLOCK), BF16)] * 2,
        grid=(count // rows,),
        in_specs=[pl.BlockSpec(memory_space=pl.ANY)] + [narrow] * 4,
        out_specs=[wide] * 2,
        compiler_params=pltpu.CompilerParams(vmem_limit_bytes=40 * 2**20),
        name="build_tables",
    )(after, weight * jnp.cos(small), weight * jnp.sin(small), cos_big, sin_big)


def fourier_kernel(spec_ref, even_ref, pick_ref, turn_ref, cos_hbm, sin_hbm, out_ref,
                   left_cos, left_sin, plus, minus, cos_ref, sin_ref, cos_sems, sin_sems):
    copies = []
    for b in range(WIDE // BLOCK):
        copies.append((
            pltpu.make_async_copy(cos_hbm.at[b], cos_ref.at[b], cos_sems.at[b]),
            pltpu.make_async_copy(sin_hbm.at[b], sin_ref.at[b], sin_sems.at[b]),
        ))
    blocks, lats, slots, channels = spec_ref.shape
    quart = channels // 4
    half = 2 * lats * quart
    for copy in copies[0] + copies[1]:
        copy.start()
    pairs = half // 2
    for j in range(blocks):
        cols = pl.ds(j * slots, slots)
        even = even_ref[pl.ds(0, 1), cols]
        for k in range(lats):
            turned = lax.dot_general(
                pick_ref[...], spec_ref[j, k], (((1,), (1,)), ((), ())),
                preferred_element_type=F32,
            )
            evens = turned * even
            odds = turned - evens
            for o, part in enumerate((evens, odds)):
                part = part.astype(BF16)
                for h in range(2):
                    rows = pl.ds(o * half + (h * lats + k) * quart, quart)
                    left_cos[rows, cols] = part[h * quart:(h + 1) * quart]
                    left_sin[rows, cols] = part[(2 + h) * quart:(3 + h) * quart]

    def product(grid):
        return (grid[:pairs] * grid[pairs:]).astype(BF16)

    for start in range(0, WIDE, BLOCK):
        cols = pl.ds(start, BLOCK)
        at = start // BLOCK
        for copy in copies[at]:
            copy.wait()
        if at + 2 < len(copies):
            for copy in copies[at + 2]:
                copy.start()
        cosines = jnp.dot(left_cos[...], cos_ref[at], preferred_element_type=F32)
        sines = jnp.dot(left_sin[...], sin_ref[at], preferred_element_type=F32)
        cos_sum = cosines[:half] + cosines[half:]
        cos_dif = cosines[:half] - cosines[half:]
        sin_sum = sines[:half] + sines[half:]
        sin_dif = sines[:half] - sines[half:]
        plus[:, cols] = product(cos_sum - sin_sum)
        minus[:, cols] = product(cos_dif - sin_dif)
        if start < QUARTER:
            first = product(cos_sum + sin_sum).reshape(lats, quart, BLOCK)
            third = product(cos_dif + sin_dif).reshape(lats, quart, BLOCK)
            out_ref[:, :, cols] = first
            out_ref[:, :, pl.ds(2 * QUARTER + start, BLOCK)] = third

    for b in range(QUARTER // 128):
        source = pl.ds(QUARTER - 128 - 128 * b, 256)
        for start, held in ((3 * QUARTER, plus), (QUARTER, minus)):
            block = jnp.dot(held[:, source], turn_ref[...], preferred_element_type=F32)
            out_ref[:, :, pl.ds(start + 128 * b, 128)] = block.astype(BF16).reshape(
                lats, quart, 128
            )


def fourier_products(spectra, order_table, cos_table, sin_table):
    blocks, lats, slots, channels = spectra.shape
    count = order_table.shape[0]
    fields = channels // 2
    even = jnp.where(order_table % 2 == 0, 1.0, 0.0).astype(F32)
    even = jnp.broadcast_to(even[None, :], (8, count))
    c = lax.iota(jnp.int32, channels)
    part, field = c // fields, c % fields
    place = part * fields + (field % 2) * (fields // 2) + field // 2
    pick = (lax.iota(jnp.int32, channels)[:, None] == place[None, :]).astype(BF16)
    turn = (lax.iota(jnp.int32, 256)[:, None] == 128 - lax.iota(jnp.int32, 128)[None, :]).astype(BF16)
    half = lats * fields
    return pl.pallas_call(
        fourier_kernel,
        out_shape=jax.ShapeDtypeStruct((lats, fields // 2, NLON), BF16),
        in_specs=[pl.BlockSpec(memory_space=pltpu.VMEM)] * 4 + [pl.BlockSpec(memory_space=pl.ANY)] * 2,
        scratch_shapes=[
            pltpu.VMEM((2 * half, count), BF16),
            pltpu.VMEM((2 * half, count), BF16),
            pltpu.VMEM((half // 2, WIDE), BF16),
            pltpu.VMEM((half // 2, WIDE), BF16),
            pltpu.VMEM((WIDE // BLOCK, count, BLOCK), BF16),
            pltpu.VMEM((WIDE // BLOCK, count, BLOCK), BF16),
            pltpu.SemaphoreType.DMA((WIDE // BLOCK,)),
            pltpu.SemaphoreType.DMA((WIDE // BLOCK,)),
        ],
        compiler_params=pltpu.CompilerParams(vmem_limit_bytes=40 * 2**20),
        name="fourier_products",
    )(spectra, even, pick, turn, cos_table, sin_table)


def local(coefficients, legendre, order_table):
    here = lax.axis_index("deg")
    y, x = here // SIDE, here % SIDE
    total, channels = coefficients.shape[0], coefficients.shape[2]
    groups = order_table.shape[0] // total
    coefficients = pltpu.with_memory_space_constraint(coefficients, pltpu.HBM)
    legendre = pltpu.with_memory_space_constraint(legendre, pltpu.HBM)
    units = ((1, SIDE), (SIDE, 1))
    state = {}
    after = legendre
    keys = [(k, way) for k in range(len(CHUNKS)) for way in range(2)]
    parts = {}
    for k, way in keys:
        place = jnp.stack([x, y] if way == 0 else [y, x]).astype(jnp.int32)
        start = way * sum(CHUNKS) + sum(CHUNKS[:k])
        parts[k, way] = legendre_sums(
            place, legendre, coefficients, after, start, CHUNKS[k], units[way]
        )
        after = parts[k, way][3]
    for k, way in keys:
        before = ((), ())
        if k:
            got = state[k - 1, way]
            before = ((got[0], after), (got[1], after))
        state[k, way] = start_sums(parts[k, way], units[way][0], before)
    tables = build_tables(order_table, after)
    tables = [pltpu.with_memory_space_constraint(t, pltpu.HBM) for t in tables]
    after = tables[0]
    for k, way in keys:
        if k:
            got = state[k - 1, way]
            before = ((got[3],), (got[2],))
        else:
            got = state[k + 1, way]
            before = ((got[0],), (got[1],))
        state[k, way], after = pass_sums(state[k, way], units[way][0], after, before)
    ends = []
    for way in range(2):
        second_phase = turn_sums if way == 0 else halve_sums
        held = [state[k, way] for k in range(len(CHUNKS))]
        end, after = second_phase(held, units[way][1], after)
        ends.append(end)
    pair = ends[0] + ends[1]
    rows = pair[0].shape[0]
    (summed,) = call(join_kernel, "join_sums", ((rows, total, channels),), after, *pair)
    sent = summed.reshape(groups, rows // groups, total, channels)
    spectra = lax.all_to_all(sent, "ord", split_axis=0, concat_axis=0, tiled=True)
    return fourier_products(spectra, order_table, *tables)


def solution(mesh):
    placed = (P("ord", "deg", None), P("ord", "deg", None), P())
    return jax.shard_map(
        local, mesh=mesh, in_specs=placed, out_specs=P(("deg", "ord"), None, None), check_vma=False
    )
```
